32 devices in a mesh: grp: 8 (over y, x, core), dev: 4 (over z).
Axes of the slice: x: 2, y: 2, z: 4, core: 2. Of those that a mesh axis runs over, the one named last changes fastest.
Arguments:
- images: float32 [2048, 1152], P(('grp', 'dev')), may hold values from -0.2 to 0.2
- texts: float32 [2048, 1152], P(('grp', 'dev')), may hold values from -0.2 to 0.2
- log_temp: float32 [1], replicated, may hold values from 1.6 to 3
- bias: float32 [1], replicated, may hold values from -3 to -1
Outputs:
- grad_images: float32 [2048, 1152], P(('grp', 'dev'))
- grad_texts: float32 [2048, 1152], P(('grp', 'dev'))
The draws below stay inside these ranges and needn't reach their ends.
All inputs are finite; a program needn't handle non-finite values.
Results may differ from the reference program's by a relative error of at most 0.0063.
Values may be sent and summed in bfloat16 or wider, within the bound.
A program may use at most 64 MiB of HBM per device.

```python
import jax
import jax.numpy as jnp
from jax import lax

D = 1152
ROWS = 64
PAIRS = 2048
N_GRP = 8
N_DEV = 4


def block_scale(key, shape, cuts, least, largest):
    factor_of, own = 1.0, jax.random.fold_in(key, 6)
    for dim, blocks in cuts:
        draws = jnp.exp(jax.random.uniform(jax.random.fold_in(own, dim), (blocks,), jnp.float32, least / len(cuts), largest / len(cuts)))
        factor_of = factor_of * jnp.repeat(draws, shape[dim] // blocks).reshape([-1 if axis == dim else 1 for axis in range(len(shape))])
    return factor_of


def bell_draw(rng, shape, scale, bound, shards=(), kind=jnp.bfloat16):
    array = jax.random.normal(rng, shape, jnp.float32) * scale
    if len(shards) > 0:
        array = block_scale(rng, shape, shards, -0.22, 0.18) * array
    return jnp.clip(array, min=-bound, max=bound).astype(kind)


def setup_inputs(seed: int = 0) -> dict:
    key_list = jax.random.split(jax.random.key(seed), 5)
    return {
        "images": bell_draw(key_list[0], (PAIRS, D), 0.03, 0.2, ((0, 32),), jnp.float32),
        "texts": bell_draw(key_list[1], (PAIRS, D), 0.03, 0.2, ((0, 32),), jnp.float32),
        "log_temp": jnp.clip(jax.random.uniform(key_list[2], (1,), jnp.float32, 1.6, 3.0), 1.6, 3.0),
        "bias": jnp.clip(jax.random.uniform(key_list[3], (1,), jnp.float32, -3.0, -1.0), -3.0, -1.0),
    }


def to_unit(raw):
    norm = jnp.sqrt(lax.optimization_barrier(jnp.sum(raw * raw, axis=1, keepdims=True)) + 1e-06)
    return (raw / norm, norm)

def from_unit(grad, unit, norm):
    return (grad - unit * lax.optimization_barrier(jnp.sum(unit * grad, axis=1, keepdims=True))) / norm

def rounded(value):
    return lax.optimization_barrier(value.astype(jnp.bfloat16)).astype(jnp.float32)

def reference(images, texts, log_temp, bias):
    temp = jnp.exp(log_temp[0])
    offset = bias[0]
    img_unit, img_norm = to_unit(images)
    txt_unit, txt_norm = to_unit(texts)
    xfull = rounded(img_unit)
    yfull = rounded(txt_unit)
    block = ROWS * N_DEV
    yblocks = yfull.reshape(N_GRP, block, D)
    row_ids = lax.broadcasted_iota(jnp.int32, (PAIRS, 1), 0)
    col_base = lax.broadcasted_iota(jnp.int32, (1, block), 1)

    def visit(dx, inputs):
        yblk, index = inputs
        dots = jnp.dot(xfull, yblk.T, precision=lax.Precision.HIGHEST)
        logits = temp * dots + offset
        cols = index * block + col_base
        delta = (row_ids == cols).astype(jnp.float32)
        coeff = rounded(jax.nn.sigmoid(logits) - delta)
        dx = dx + jnp.dot(coeff, yblk, precision=lax.Precision.HIGHEST)
        dy = jnp.dot(coeff.T, xfull, precision=lax.Precision.HIGHEST)
        return (dx, dy)
    indices = jnp.arange(N_GRP, dtype=jnp.int32)
    dx, dys = lax.scan(visit, jnp.zeros((PAIRS, D), jnp.float32), (yblocks, indices))
    dx = temp * dx
    dy = temp * dys.reshape(PAIRS, D)
    return (from_unit(dx, img_unit, img_norm), from_unit(dy, txt_unit, txt_norm))
```

```python
import functools

import jax
import jax.numpy as jnp
from jax import lax
from jax.experimental import pallas as pl
from jax.experimental.pallas import tpu as pltpu
from jax.sharding import PartitionSpec as P

NT = (((1,), (1,)), ((), ()))
TN = (((0,), (0,)), ((), ()))


def dot(a, b, dims=(((1,), (0,)), ((), ()))):
    return lax.dot_general(a, b, dims, preferred_element_type=jnp.float32)


def to_unit(raw):
    norm = jnp.sqrt(jnp.sum(raw * raw, axis=1, keepdims=True) + 1e-06)
    return (raw / norm, norm)


def from_unit(grad, unit, norm):
    return (grad - unit * jnp.sum(unit * grad, axis=1, keepdims=True)) / norm


def flipped(index, mask):
    out, bit = index, 1
    while bit <= mask:
        if mask & bit:
            out = out + bit - 2 * bit * ((index // bit) % 2)
        bit *= 2
    return out


def kernel(
    groups, members,
    log_temp_ref, bias_ref, img_ref, txt_ref, grad_img_ref, grad_txt_ref,
    x, y, coeff, dx, dx_out, dx_in, dy_sib, dy_mine, dy_in, dy_out, dy_home,
    x_send, x_recv, y_send, y_recv, sib_send, sib_recv,
    dx_send, dx_recv, dys_send, dys_recv, dyo_send, dyo_recv,
):
    rows, width = img_ref.shape
    chips = groups // 2
    tree = members == 4
    grp = lax.axis_index("grp")
    me = lax.axis_index("dev")
    core = grp % 2
    chip = grp // 2
    sibling = {"grp": grp + 1 - 2 * core}

    def peer(k):
        return {"grp": 2 * flipped(chip, k) + core}

    def block(index):
        return pl.ds(pl.multiple_of(index * rows, rows), rows)

    def remote(src, dst, send, recv, device):
        return pltpu.make_async_remote_copy(
            src_ref=src, dst_ref=dst, send_sem=send, recv_sem=recv,
            device_id=device, device_id_type=pl.DeviceIdType.MESH,
        )

    barrier = pltpu.get_barrier_semaphore()
    for k in range(1, chips):
        pl.semaphore_signal(barrier, device_id=peer(k), device_id_type=pl.DeviceIdType.MESH)
    pl.semaphore_signal(barrier, device_id=sibling, device_id_type=pl.DeviceIdType.MESH)
    for k in range(1, members):
        pl.semaphore_signal(
            barrier, device_id={"dev": (me + k) % members}, device_id_type=pl.DeviceIdType.MESH
        )

    img_unit, img_norm = to_unit(img_ref[...])
    x[block(me), :] = img_unit.astype(jnp.bfloat16)
    txt_unit, txt_norm = to_unit(txt_ref[...])
    y[core, block(chip), :] = txt_unit.astype(jnp.bfloat16)
    temp = jnp.exp(jnp.full((1, 1), log_temp_ref[0], jnp.float32))
    offset = bias_ref[0]

    pl.semaphore_wait(barrier, chips + members - 1)

    side = me // 2
    pair = flipped(me, 1)
    across = 2 - side
    far = 3 - 3 * side
    inner = jnp.logical_or(me == 1, me == 2)

    def send_x(source, slot, device):
        held = x.at[block(source), :]
        return remote(held, held, x_send.at[slot], x_recv.at[source], {"dev": device})

    def send_y(k, owner):
        held = y.at[core, block(owner), :]
        return remote(held, held, y_send.at[k], y_recv.at[k], peer(k))

    def share_y(k, half):
        held = y.at[half, block(flipped(chip, k)), :]
        return remote(held, held, sib_send.at[k], sib_recv.at[k], sibling)

    if tree:
        own_x = [send_x(me, 0, pair), send_x(me, 1, across)]
    else:
        own_x = [send_x(me, k - 1, (me + k) % members) for k in range(1, members)]
    own_y = [send_y(k, chip) for k in range(1, chips)]
    for copy in own_x[:1] + own_y + own_x[1:]:
        copy.start()
    share_y(0, core).start()

    def relay(slot, source):
        @pl.when(inner)
        def _():
            send_x(source, 0, pair).wait_recv()
            send_x(source, slot, pair).start()

    for k in range(1, chips):
        if tree and k == chips - 1:
            relay(2, across)
        send_y(k, flipped(chip, k)).wait_recv()
        share_y(k, core).start()
    if tree:
        relay(3, far)
    for k in range(chips):
        share_y(k, 1 - core).wait_recv()

    row_ids = lax.broadcasted_iota(jnp.int32, (rows, chips * rows), 0)
    col_ids = lax.broadcasted_iota(jnp.int32, (rows, chips * rows), 1)
    diagonal = col_ids == row_ids + chip * rows

    def score(source):
        mine = x[block(source), :]
        total = None
        for half in range(2):
            texts = y[half]
            logits = temp * dot(mine, texts, NT) + offset
            own = jnp.logical_and(source == me, core == half)
            hits = jnp.where(jnp.logical_and(diagonal, own), 1.0, 0.0)
            part = (jax.nn.sigmoid(logits) - hits).astype(jnp.bfloat16)
            coeff[half, block(source), :] = part
            term = dot(part, texts)
            total = term if total is None else total + term
        dx[source] = total

    def await_x(source):
        send_x(source, 0, me).wait_recv()

    def send_dx(dest, device, slot, into):
        return remote(
            dx_out.at[dest], dx_in.at[into], dx_send.at[slot], dx_recv.at[into], {"dev": device}
        )

    def ship_dx(dest, device, slot, into, value):
        dx_out[dest] = value.astype(jnp.bfloat16)
        send_dx(dest, device, slot, into).start()

    if tree:
        @pl.when(jnp.logical_not(inner))
        def _():
            await_x(pair)
        @pl.when(inner)
        def _():
            await_x(pair)
        score(pair)
        ship_dx(pair, pair, 0, 0, dx[pair])

        @pl.when(jnp.logical_not(inner))
        def _():
            await_x(across)
            score(across)
            ship_dx(across, pair, 1, 2, dx[across])
            score(me)
            await_x(far)
            score(far)
            ship_dx(far, pair, 2, 3, dx[far])

        @pl.when(inner)
        def _():
            score(across)
            score(far)
            score(me)
    else:
        def direct(k, carry):
            source = (me + k) % members

            @pl.when(k > 0)
            def _():
                await_x(source)
            score(source)

            @pl.when(k > 0)
            def _():
                ship_dx(source, source, k - 1, k - 1, dx[source])
            return carry
        lax.fori_loop(0, members, direct, 0)

    def share_dy(k):
        held = block(flipped(chip, k))
        return remote(
            dy_sib.at[held, :], dy_in.at[held, :], dys_send.at[k], dys_recv.at[k], sibling
        )

    def send_dy(k):
        return remote(dy_out.at[k], dy_home.at[k], dyo_send.at[k], dyo_recv.at[k], peer(k))

    images = x[...]
    dy_sib[...] = dot(coeff[1 - core], images, TN).astype(jnp.bfloat16)
    order = list(range(chips - 1, -1, -1))
    for k in order:
        share_dy(k).start()
    dy_mine[...] = dot(coeff[core], images, TN)
    for k in order:
        share_dy(k).wait_recv()
        if k > 0:
            held = block(flipped(chip, k))
            summed = dy_mine[held, :] + dy_in[held, :].astype(jnp.float32)
            dy_out[k] = summed.astype(jnp.bfloat16)
            send_dy(k).start()

    if tree:
        @pl.when(inner)
        def _():
            for dest, into in ((across, 2), (far, 3)):
                send_dx(dest, dest, 0, into).wait_recv()
                ship_dx(dest, dest, into - 1, 1, dx[dest] + dx_in[into].astype(jnp.float32))

    total = dx[me]
    for into in range(2 if tree else members - 1):
        send_dx(me, me, 0, into).wait_recv()
        total = total + dx_in[into].astype(jnp.float32)
    grad_img_ref[...] = from_unit(temp * total, img_unit, img_norm)

    total = dy_mine[block(chip), :] + dy_in[block(chip), :].astype(jnp.float32)
    for k in range(1, chips):
        send_dy(k).wait_recv()
        total = total + dy_home[k].astype(jnp.float32)
    grad_txt_ref[...] = from_unit(temp * total, txt_unit, txt_norm)

    for copy in own_x + own_y:
        copy.wait_send()
    for k in range(chips):
        share_y(k, core).wait_send()
        share_dy(k).wait_send()
        if k > 0:
            send_dy(k).wait_send()
    if tree:
        for slot in range(3):
            send_dx(me, me, slot, 0).wait_send()

        @pl.when(inner)
        def _():
            send_x(across, 2, pair).wait_send()
            send_x(far, 3, pair).wait_send()
    else:
        for slot in range(members - 1):
            send_dx(me, me, slot, 0).wait_send()


def on_device(groups, members, images, texts, log_temp, bias):
    rows, width = images.shape
    chips = groups // 2
    half = chips * rows
    f32, bf16, dma = jnp.float32, jnp.bfloat16, pltpu.SemaphoreType.DMA
    vmem = pl.BlockSpec(memory_space=pltpu.VMEM)
    smem = pl.BlockSpec(memory_space=pltpu.SMEM)
    return pl.pallas_call(
        functools.partial(kernel, groups, members),
        out_shape=(jax.ShapeDtypeStruct((rows, width), f32),) * 2,
        in_specs=[smem, smem, vmem, vmem],
        out_specs=(vmem, vmem),
        scratch_shapes=[
            pltpu.VMEM((members * rows, width), bf16),
            pltpu.VMEM((2, half, width), bf16),
            pltpu.VMEM((2, members * rows, half), bf16),
            pltpu.VMEM((members, rows, width), f32),
            pltpu.VMEM((members, rows, width), bf16),
            pltpu.VMEM((max(members, 4), rows, width), bf16),
            pltpu.VMEM((half, width), bf16),
            pltpu.VMEM((half, width), f32),
            pltpu.VMEM((half, width), bf16),
            pltpu.VMEM((chips, rows, width), bf16),
            pltpu.VMEM((chips, rows, width), bf16),
            dma((max(members, 4),)), dma((members,)),
            dma((chips,)), dma((chips,)), dma((chips,)), dma((chips,)),
            dma((max(members, 4),)), dma((max(members, 4),)),
            dma((chips,)), dma((chips,)), dma((chips,)), dma((chips,)),
        ],
        compiler_params=pltpu.CompilerParams(
            collective_id=0, has_side_effects=True, vmem_limit_bytes=48 * 2**20
        ),
        cost_estimate=pl.CostEstimate(
            flops=12 * half * members * rows * width,
            bytes_accessed=16 * rows * width,
            transcendentals=2 * half * members * rows,
        ),
    )(log_temp, bias, images, texts)


def solution(mesh):
    placed = P(("grp", "dev"), None)
    return jax.shard_map(
        functools.partial(on_device, mesh.shape["grp"], mesh.shape["dev"]),
        mesh=mesh,
        in_specs=(placed, placed, P(), P()),
        out_specs=(placed, placed),
        check_vma=False,
    )
```

```python
import functools

import jax
import jax.numpy as jnp
from jax import lax
from jax.experimental import pallas as pl
from jax.experimental.pallas import tpu as pltpu
from jax.sharding import PartitionSpec as P

PARTS = 2
NT = (((1,), (1,)), ((), ()))
TN = (((0,), (0,)), ((), ()))


def dot(a, b, dims=(((1,), (0,)), ((), ()))):
    return lax.dot_general(a, b, dims, preferred_element_type=jnp.float32)


def to_unit(raw):
    norm = jnp.sqrt(jnp.sum(raw * raw, axis=1, keepdims=True) + 1e-06)
    return (raw / norm, norm)


def from_unit(grad, unit, norm):
    return (grad - unit * jnp.sum(unit * grad, axis=1, keepdims=True)) / norm


def flipped(index, mask):
    out, bit = index, 1
    while bit <= mask:
        if mask & bit:
            out = out + bit - 2 * bit * ((index // bit) % 2)
        bit *= 2
    return out


def kernel(
    groups, members,
    log_temp_ref, bias_ref, img_hbm, txt_hbm, grad_img_ref, grad_txt_ref,
    img_ref, txt_ref, load_sem, x, y, coeff, dx, dx_out, dx_in, dy_sib, dy_mine, dy_in, dy_out, dy_home,
    x_send, x_recv, y_send, y_recv, sib_send, sib_recv,
    dx_send, dx_recv, dys_send, dys_recv, dyo_send, dyo_recv,
):
    rows, width = img_ref.shape
    chips = groups // 2
    tree = members == 4
    grp = lax.axis_index("grp")
    me = lax.axis_index("dev")
    core = grp % 2
    chip = grp // 2
    sibling = {"grp": grp + 1 - 2 * core}
    part = rows // PARTS
    load_img = pltpu.make_async_copy(img_hbm, img_ref, load_sem.at[0])
    load_txt = pltpu.make_async_copy(txt_hbm, txt_ref, load_sem.at[1])
    load_img.start()
    load_txt.start()

    def peer(k):
        return {"grp": 2 * flipped(chip, k) + core}

    def block(index):
        return pl.ds(pl.multiple_of(index * rows, rows), rows)

    def piece(index, c):
        return pl.ds(pl.multiple_of(index * rows + c * part, part), part)

    def remote(src, dst, send, recv, device):
        return pltpu.make_async_remote_copy(
            src_ref=src, dst_ref=dst, send_sem=send, recv_sem=recv,
            device_id=device, device_id_type=pl.DeviceIdType.MESH,
        )

    barrier = pltpu.get_barrier_semaphore()
    for k in range(1, chips):
        pl.semaphore_signal(barrier, device_id=peer(k), device_id_type=pl.DeviceIdType.MESH)
    pl.semaphore_signal(barrier, device_id=sibling, device_id_type=pl.DeviceIdType.MESH)
    for k in range(1, members):
        pl.semaphore_signal(
            barrier, device_id={"dev": (me + k) % members}, device_id_type=pl.DeviceIdType.MESH
        )

    load_img.wait()
    img_unit, img_norm = to_unit(img_ref[...])
    x[block(me), :] = img_unit.astype(jnp.bfloat16)
    load_txt.wait()
    txt_unit, txt_norm = to_unit(txt_ref[...])
    y[core, block(chip), :] = txt_unit.astype(jnp.bfloat16)
    temp = jnp.exp(jnp.full((1, 1), log_temp_ref[0], jnp.float32))
    offset = bias_ref[0]

    pl.semaphore_wait(barrier, chips + members - 1)

    side = me // 2
    pair = flipped(me, 1)
    across = 2 - side
    far = 3 - 3 * side
    inner = jnp.logical_or(me == 1, me == 2)

    def send_x(source, c, slot, device):
        held = x.at[piece(source, c), :]
        return remote(held, held, x_send.at[slot, c], x_recv.at[source, c], {"dev": device})

    def send_y(k, owner):
        held = y.at[core, block(owner), :]
        return remote(held, held, y_send.at[k], y_recv.at[k], peer(k))

    def share_y(k, half):
        held = y.at[half, block(flipped(chip, k)), :]
        return remote(held, held, sib_send.at[k], sib_recv.at[k], sibling)

    own_y = [send_y(k, chip) for k in range(1, chips)]
    if tree:
        own_x = [send_x(me, c, 0, pair) for c in range(PARTS)]
        for copy in own_x:
            copy.start()

        @pl.when(inner)
        def _():
            for c in range(PARTS):
                send_x(me, c, 1, across).start()
    else:
        own_x = [
            send_x(me, c, k - 1, (me + k) % members) for k in range(1, members) for c in range(PARTS)
        ]
        for copy in own_x:
            copy.start()
    for copy in own_y:
        copy.start()
    share_y(0, core).start()

    def relay_x(*steps):
        @pl.when(inner)
        def _():
            for source, c, slot, device in steps:
                send_x(source, c, 0, device).wait_recv()
                send_x(source, c, slot, device).start()

    def relay_y(k):
        send_y(k, flipped(chip, k)).wait_recv()
        share_y(k, core).start()

    if tree:
        for c in range(PARTS):
            relay_x((pair, c, 2, across), (across, c, 3, pair))
        relay_x((far, 0, 4, pair))
    for k in range(1, chips - 1):
        relay_y(k)
    if tree:
        relay_x(*((far, c, 4, pair) for c in range(1, PARTS)))
    relay_y(chips - 1)
    for k in range(chips):
        share_y(k, 1 - core).wait_recv()

    def score(first, count):
        extent = count * rows
        span = pl.ds(pl.multiple_of(first * rows, rows), extent)
        row_ids = lax.broadcasted_iota(jnp.int32, (extent, chips * rows), 0) + (first - me) * rows
        col_ids = lax.broadcasted_iota(jnp.int32, (extent, chips * rows), 1) - chip * rows
        mine = x[span, :]
        total = None
        for half in range(2):
            texts = y[half]
            logits = temp * dot(mine, texts, NT) + offset
            hits = (row_ids == col_ids) & (row_ids >= 0) & (row_ids < rows) & (core == half)
            coeffs = (jax.nn.sigmoid(logits) - jnp.where(hits, 1.0, 0.0)).astype(jnp.bfloat16)
            coeff[half, span, :] = coeffs
            term = dot(coeffs, texts)
            total = term if total is None else total + term
        dx[span, :] = total

    def await_x(source):
        for c in range(PARTS):
            send_x(source, c, 0, me).wait_recv()

    def send_dx(dest, c, device, slot, into):
        return remote(
            dx_out.at[piece(dest, c), :], dx_in.at[into, pl.ds(c * part, part), :],
            dx_send.at[slot, c], dx_recv.at[into, c], {"dev": device},
        )

    def ship_dx(dest, device, slot, into, c, value):
        dx_out[piece(dest, c), :] = value.astype(jnp.bfloat16)
        send_dx(dest, c, device, slot, into).start()

    def ship_own(dest, device, slot, into):
        for c in range(PARTS):
            ship_dx(dest, device, slot, into, c, dx[piece(dest, c), :])

    if tree:
        @pl.when(jnp.logical_not(inner))
        def _():
            await_x(pair)
            await_x(across)
            score(side, 3)
            ship_own(pair, pair, 0, 0)
            ship_own(across, pair, 1, 2)
            await_x(far)
            score(far, 1)
            ship_own(far, pair, 2, 3)

        @pl.when(inner)
        def _():
            score(0, 4)
            ship_own(pair, pair, 0, 0)
    else:
        def direct(k, carry):
            source = (me + k) % members

            @pl.when(k > 0)
            def _():
                await_x(source)
            score(source, 1)

            @pl.when(k > 0)
            def _():
                ship_own(source, source, k - 1, k - 1)
            return carry
        lax.fori_loop(0, members, direct, 0)

    def share_dy(k):
        held = block(flipped(chip, k))
        return remote(
            dy_sib.at[held, :], dy_in.at[held, :], dys_send.at[k], dys_recv.at[k], sibling
        )

    def send_dy(k):
        return remote(dy_out.at[k], dy_home.at[k], dyo_send.at[k], dyo_recv.at[k], peer(k))

    images = x[...]
    dy_sib[...] = dot(coeff[1 - core], images, TN).astype(jnp.bfloat16)
    order = list(range(chips - 1, -1, -1))
    for k in order:
        share_dy(k).start()
    dy_mine[...] = dot(coeff[core], images, TN)
    for k in order:
        share_dy(k).wait_recv()
        if k > 0:
            held = block(flipped(chip, k))
            summed = dy_mine[held, :] + dy_in[held, :].astype(jnp.float32)
            dy_out[k] = summed.astype(jnp.bfloat16)
            send_dy(k).start()

    if tree:
        @pl.when(inner)
        def _():
            for dest, into in ((across, 2), (far, 3)):
                for c in range(PARTS):
                    send_dx(dest, c, dest, 0, into).wait_recv()
                    passed = dx_in[into, pl.ds(c * part, part), :].astype(jnp.float32)
                    ship_dx(dest, dest, into - 1, 1, c, dx[piece(dest, c), :] + passed)

    total = dx[block(me), :]
    for into in range(2 if tree else members - 1):
        for c in range(PARTS):
            send_dx(me, c, me, 0, into).wait_recv()
        total = total + dx_in[into].astype(jnp.float32)
    grad_img_ref[...] = from_unit(temp * total, img_unit, img_norm)

    total = dy_mine[block(chip), :] + dy_in[block(chip), :].astype(jnp.float32)
    for k in range(1, chips):
        send_dy(k).wait_recv()
        total = total + dy_home[k].astype(jnp.float32)
    grad_txt_ref[...] = from_unit(temp * total, txt_unit, txt_norm)

    for copy in own_x + own_y:
        copy.wait_send()
    for k in range(chips):
        share_y(k, core).wait_send()
        share_dy(k).wait_send()
        if k > 0:
            send_dy(k).wait_send()
    for slot in range(3 if tree else members - 1):
        for c in range(PARTS):
            send_dx(me, c, me, slot, 0).wait_send()
    if tree:
        @pl.when(inner)
        def _():
            for c in range(PARTS):
                for slot in range(1, 5):
                    send_x(me, c, slot, pair).wait_send()


def on_device(groups, members, images, texts, log_temp, bias):
    rows, width = images.shape
    chips = groups // 2
    half = chips * rows
    f32, bf16, dma = jnp.float32, jnp.bfloat16, pltpu.SemaphoreType.DMA
    vmem = pl.BlockSpec(memory_space=pltpu.VMEM)
    hbm = pl.BlockSpec(memory_space=pltpu.HBM)
    smem = pl.BlockSpec(memory_space=pltpu.SMEM)
    return pl.pallas_call(
        functools.partial(kernel, groups, members),
        out_shape=(jax.ShapeDtypeStruct((rows, width), f32),) * 2,
        in_specs=[smem, smem, hbm, hbm],
        out_specs=(vmem, vmem),
        scratch_shapes=[
            pltpu.VMEM((rows, width), f32),
            pltpu.VMEM((rows, width), f32),
            dma((2,)),
            pltpu.VMEM((members * rows, width), bf16),
            pltpu.VMEM((2, half, width), bf16),
            pltpu.VMEM((2, members * rows, half), bf16),
            pltpu.VMEM((members * rows, width), f32),
            pltpu.VMEM((members * rows, width), bf16),
            pltpu.VMEM((max(members, 4), rows, width), bf16),
            pltpu.VMEM((half, width), bf16),
            pltpu.VMEM((half, width), f32),
            pltpu.VMEM((half, width), bf16),
            pltpu.VMEM((chips, rows, width), bf16),
            pltpu.VMEM((chips, rows, width), bf16),
            dma((max(members, 5), PARTS)), dma((members, PARTS)),
            dma((chips,)), dma((chips,)), dma((chips,)), dma((chips,)),
            dma((max(members, 4), PARTS)), dma((max(members, 4), PARTS)),
            dma((chips,)), dma((chips,)), dma((chips,)), dma((chips,)),
        ],
        compiler_params=pltpu.CompilerParams(
            collective_id=0, has_side_effects=True, vmem_limit_bytes=48 * 2**20
        ),
        cost_estimate=pl.CostEstimate(
            flops=12 * half * members * rows * width,
            bytes_accessed=16 * rows * width,
            transcendentals=2 * half * members * rows,
        ),
    )(log_temp, bias, images, texts)


def solution(mesh):
    placed = P(("grp", "dev"), None)
    return jax.shard_map(
        functools.partial(on_device, mesh.shape["grp"], mesh.shape["dev"]),
        mesh=mesh,
        in_specs=(placed, placed, P(), P()),
        out_specs=(placed, placed),
        check_vma=False,
    )
```

```python
import functools

import jax
import jax.numpy as jnp
from jax import lax
from jax.experimental import pallas as pl
from jax.experimental.pallas import tpu as pltpu
from jax.sharding import PartitionSpec as P

PARTS = 2
NT = (((1,), (1,)), ((), ()))
TN = (((0,), (0,)), ((), ()))


def dot(a, b, dims=(((1,), (0,)), ((), ()))):
    return lax.dot_general(a, b, dims, preferred_element_type=jnp.float32)


def to_unit(raw):
    norm = jnp.sqrt(jnp.sum(raw * raw, axis=1, keepdims=True) + 1e-06)
    return (raw / norm, norm)


def from_unit(grad, unit, norm):
    return (grad - unit * jnp.sum(unit * grad, axis=1, keepdims=True)) / norm


def flipped(index, mask):
    out, bit = index, 1
    while bit <= mask:
        if mask & bit:
            out = out + bit - 2 * bit * ((index // bit) % 2)
        bit *= 2
    return out


def kernel(
    groups, members,
    log_temp_ref, bias_ref, img_hbm, txt_hbm, grad_img_ref, grad_txt_ref,
    img_ref, txt_ref, load_sem, x, y, coeff, dx, dx_out, dx_in, dy_sib, dy_mine, dy_in, dy_out, dy_home,
    x_send, x_recv, y_send, y_recv, sib_send, sib_recv,
    dx_send, dx_recv, dys_send, dys_recv, dyo_send, dyo_recv,
):
    rows, width = img_ref.shape
    chips = groups // 2
    tree = members == 4
    grp = lax.axis_index("grp")
    me = lax.axis_index("dev")
    core = grp % 2
    chip = grp // 2
    sibling = {"grp": grp + 1 - 2 * core}
    part = rows // PARTS
    load_img = pltpu.make_async_copy(img_hbm, img_ref, load_sem.at[0])
    load_txt = pltpu.make_async_copy(txt_hbm, txt_ref, load_sem.at[1])
    load_img.start()
    load_txt.start()

    def peer(k):
        return {"grp": 2 * flipped(chip, k) + core}

    def block(index):
        return pl.ds(pl.multiple_of(index * rows, rows), rows)

    def piece(index, c):
        return pl.ds(pl.multiple_of(index * rows + c * part, part), part)

    def remote(src, dst, send, recv, device):
        return pltpu.make_async_remote_copy(
            src_ref=src, dst_ref=dst, send_sem=send, recv_sem=recv,
            device_id=device, device_id_type=pl.DeviceIdType.MESH,
        )

    barrier = pltpu.get_barrier_semaphore()
    for k in range(1, chips):
        pl.semaphore_signal(barrier, device_id=peer(k), device_id_type=pl.DeviceIdType.MESH)
    pl.semaphore_signal(barrier, device_id=sibling, device_id_type=pl.DeviceIdType.MESH)
    for k in range(1, members):
        pl.semaphore_signal(
            barrier, device_id={"dev": (me + k) % members}, device_id_type=pl.DeviceIdType.MESH
        )

    load_img.wait()
    img_unit, img_norm = to_unit(img_ref[...])
    x[block(me), :] = img_unit.astype(jnp.bfloat16)
    load_txt.wait()
    txt_unit, txt_norm = to_unit(txt_ref[...])
    y[core, block(chip), :] = txt_unit.astype(jnp.bfloat16)
    temp = jnp.exp(jnp.full((1, 1), log_temp_ref[0], jnp.float32))
    offset = bias_ref[0]

    pl.semaphore_wait(barrier, chips + members - 1)

    side = me // 2
    pair = flipped(me, 1)
    across = 2 - side
    far = 3 - 3 * side
    inner = jnp.logical_or(me == 1, me == 2)

    def send_x(source, c, slot, device):
        held = x.at[piece(source, c), :]
        return remote(held, held, x_send.at[slot, c], x_recv.at[source, c], {"dev": device})

    def send_y(k, owner):
        held = y.at[core, block(owner), :]
        return remote(held, held, y_send.at[k], y_recv.at[k], peer(k))

    def share_y(k, half):
        held = y.at[half, block(flipped(chip, k)), :]
        return remote(held, held, sib_send.at[k], sib_recv.at[k], sibling)

    own_y = [send_y(k, chip) for k in range(1, chips)]
    if tree:
        own_x = [send_x(me, c, 0, pair) for c in range(PARTS)]
        for copy in own_x:
            copy.start()

        @pl.when(inner)
        def _():
            for c in range(PARTS):
                send_x(me, c, 1, across).start()
    else:
        own_x = [
            send_x(me, c, k - 1, (me + k) % members) for k in range(1, members) for c in range(PARTS)
        ]
        for copy in own_x:
            copy.start()
    for copy in own_y:
        copy.start()
    share_y(0, core).start()

    def relay_x(*steps):
        @pl.when(inner)
        def _():
            for source, c, slot, device in steps:
                send_x(source, c, 0, device).wait_recv()
                send_x(source, c, slot, device).start()

    def relay_y(k):
        send_y(k, flipped(chip, k)).wait_recv()
        share_y(k, core).start()

    if tree:
        for c in range(PARTS):
            relay_x((pair, c, 2, across), (across, c, 3, pair))
        relay_x((far, 0, 4, pair))
    for k in range(1, chips - 1):
        relay_y(k)
    if tree:
        relay_x(*((far, c, 4, pair) for c in range(1, PARTS)))
    relay_y(chips - 1)
    for k in range(chips):
        share_y(k, 1 - core).wait_recv()

    def score(first, count):
        extent = count * rows
        span = pl.ds(pl.multiple_of(first * rows, rows), extent)
        row_ids = lax.broadcasted_iota(jnp.int32, (extent, chips * rows), 0) + (first - me) * rows
        col_ids = lax.broadcasted_iota(jnp.int32, (extent, chips * rows), 1) - chip * rows
        mine = x[span, :]
        total = None
        for half in range(2):
            texts = y[half]
            logits = temp * dot(mine, texts, NT) + offset
            hits = (row_ids == col_ids) & (row_ids >= 0) & (row_ids < rows) & (core == half)
            coeffs = (jax.nn.sigmoid(logits) - jnp.where(hits, 1.0, 0.0)).astype(jnp.bfloat16)
            coeff[half, span, :] = coeffs
            term = dot(coeffs, texts)
            total = term if total is None else total + term
        dx[span, :] = total

    def await_x(source):
        for c in range(PARTS):
            send_x(source, c, 0, me).wait_recv()

    def send_dx(dest, c, device, slot, into):
        return remote(
            dx_out.at[piece(dest, c), :], dx_in.at[into, pl.ds(c * part, part), :],
            dx_send.at[slot, c], dx_recv.at[into, c], {"dev": device},
        )

    def ship_dx(dest, device, slot, into, c, value):
        dx_out[piece(dest, c), :] = value.astype(jnp.bfloat16)
        send_dx(dest, c, device, slot, into).start()

    def ship_own(dest, device, slot, into):
        for c in range(PARTS):
            ship_dx(dest, device, slot, into, c, dx[piece(dest, c), :])

    if tree:
        @pl.when(jnp.logical_not(inner))
        def _():
            await_x(pair)
            await_x(across)
            score(side, 3)
            ship_own(pair, pair, 0, 0)
            ship_own(across, pair, 1, 2)
            await_x(far)
            score(far, 1)
            ship_own(far, pair, 2, 3)

        @pl.when(inner)
        def _():
            score(0, 4)
            ship_own(pair, pair, 0, 0)
    else:
        def direct(k, carry):
            source = (me + k) % members

            @pl.when(k > 0)
            def _():
                await_x(source)
            score(source, 1)

            @pl.when(k > 0)
            def _():
                ship_own(source, source, k - 1, k - 1)
            return carry
        lax.fori_loop(0, members, direct, 0)

    def share_dy(k):
        held = block(flipped(chip, k))
        return remote(
            dy_sib.at[held, :], dy_in.at[held, :], dys_send.at[k], dys_recv.at[k], sibling
        )

    def send_dy(k):
        return remote(dy_out.at[k], dy_home.at[k], dyo_send.at[k], dyo_recv.at[k], peer(k))

    images = x[...]
    dy_sib[...] = dot(coeff[1 - core], images, TN).astype(jnp.bfloat16)
    order = list(range(chips - 1, -1, -1))
    for k in order:
        share_dy(k).start()
    dy_mine[...] = dot(coeff[core], images, TN)
    for k in order:
        share_dy(k).wait_recv()
        if k > 0:
            held = block(flipped(chip, k))
            summed = dy_mine[held, :] + dy_in[held, :].astype(jnp.float32)
            dy_out[k] = summed.astype(jnp.bfloat16)
            send_dy(k).start()

    if tree:
        @pl.when(inner)
        def _():
            for dest, into in ((across, 2), (far, 3)):
                for c in range(PARTS):
                    send_dx(dest, c, dest, 0, into).wait_recv()
                    passed = dx_in[into, pl.ds(c * part, part), :].astype(jnp.float32)
                    ship_dx(dest, dest, into - 1, 1, c, dx[piece(dest, c), :] + passed)

    total = dx[block(me), :]
    for into in range(2 if tree else members - 1):
        for c in range(PARTS):
            send_dx(me, c, me, 0, into).wait_recv()
        total = total + dx_in[into].astype(jnp.float32)
    grad_img_ref[...] = from_unit(temp * total, img_unit, img_norm)

    total = dy_mine[block(chip), :] + dy_in[block(chip), :].astype(jnp.float32)
    for k in range(1, chips):
        send_dy(k).wait_recv()
        total = total + dy_home[k].astype(jnp.float32)
    grad_txt_ref[...] = from_unit(temp * total, txt_unit, txt_norm)

    for copy in own_x + own_y:
        copy.wait_send()
    for k in range(chips):
        share_y(k, core).wait_send()
        share_dy(k).wait_send()
        if k > 0:
            send_dy(k).wait_send()
    for slot in range(3 if tree else members - 1):
        for c in range(PARTS):
            send_dx(me, c, me, slot, 0).wait_send()
    if tree:
        @pl.when(inner)
        def _():
            for c in range(PARTS):
                for slot in range(1, 5):
                    send_x(me, c, slot, pair).wait_send()


def on_device(groups, members, images, texts, log_temp, bias):
    rows, width = images.shape
    chips = groups // 2
    half = chips * rows
    f32, bf16, dma = jnp.float32, jnp.bfloat16, pltpu.SemaphoreType.DMA
    vmem = pl.BlockSpec(memory_space=pltpu.VMEM)
    hbm = pl.BlockSpec(memory_space=pltpu.HBM)
    smem = pl.BlockSpec(memory_space=pltpu.SMEM)
    return pl.pallas_call(
        functools.partial(kernel, groups, members),
        out_shape=(jax.ShapeDtypeStruct((rows, width), f32),) * 2,
        in_specs=[smem, smem, hbm, hbm],
        out_specs=(vmem, vmem),
        scratch_shapes=[
            pltpu.VMEM((rows, width), f32),
            pltpu.VMEM((rows, width), f32),
            dma((2,)),
            pltpu.VMEM((members * rows, width), bf16),
            pltpu.VMEM((2, half, width), bf16),
            pltpu.VMEM((2, members * rows, half), bf16),
            pltpu.VMEM((members * rows, width), f32),
            pltpu.VMEM((members * rows, width), bf16),
            pltpu.VMEM((max(members, 4), rows, width), bf16),
            pltpu.VMEM((half, width), bf16),
            pltpu.VMEM((half, width), f32),
            pltpu.VMEM((half, width), bf16),
            pltpu.VMEM((chips, rows, width), bf16),
            pltpu.VMEM((chips, rows, width), bf16),
            dma((max(members, 5), PARTS)), dma((members, PARTS)),
            dma((chips,)), dma((chips,)), dma((chips,)), dma((chips,)),
            dma((max(members, 4), PARTS)), dma((max(members, 4), PARTS)),
            dma((chips,)), dma((chips,)), dma((chips,)), dma((chips,)),
        ],
        compiler_params=pltpu.CompilerParams(
            collective_id=0, has_side_effects=True, vmem_limit_bytes=54400 * 2**10
        ),
        cost_estimate=pl.CostEstimate(
            flops=12 * half * members * rows * width,
            bytes_accessed=16 * rows * width,
            transcendentals=2 * half * members * rows,
        ),
    )(log_temp, bias, images, texts)


def solution(mesh):
    placed = P(("grp", "dev"), None)
    return jax.shard_map(
        functools.partial(on_device, mesh.shape["grp"], mesh.shape["dev"]),
        mesh=mesh,
        in_specs=(placed, placed, P(), P()),
        out_specs=(placed, placed),
        check_vma=False,
    )
```
